32 devices in a mesh: replica: 4 (over z), mp: 4 (over y, x), refresh: 2 (over core).
Axes of the slice: x: 2, y: 2, z: 4, core: 2. Of those that a mesh axis runs over, the one named last changes fastest.
Arguments:
- grad_partial: bfloat16 [4, 2, 512, 2048], P('replica', 'refresh', 'mp'), may hold values from -252 to 252
- left_stats: float32 [2, 512, 2048], P('refresh', 'replica', 'mp'), may hold values from -4608 to 5120, as said below
- right_stats: float32 [2, 512, 2048], P('refresh', 'replica', 'mp'), may hold values from -4608 to 5120, as said below
- left_roots: float32 [2, 512, 2048], P('refresh', 'replica', 'mp'), may hold values from -1 to 1, as said below
- right_roots: float32 [2, 512, 2048], P('refresh', 'replica', 'mp'), may hold values from -1 to 1, as said below
- newton_counts: int32 [2, 4], replicated, may hold values from 1 to 4
- owner: int32 [2, 4], replicated, may hold values from 0 to 3, each once within a row
Outputs:
- update: float32 [2, 512, 2048], P('refresh', 'mp')
- new_left_stats: float32 [2, 512, 2048], P('refresh', 'replica', 'mp')
- new_right_stats: float32 [2, 512, 2048], P('refresh', 'replica', 'mp')
- new_left_roots: float32 [2, 512, 2048], P('refresh', 'replica', 'mp')
- new_right_roots: float32 [2, 512, 2048], P('refresh', 'replica', 'mp')
The draws below stay inside these ranges and needn't reach their ends.
Inputs may be any that keep to these rules, and one draw needn't show every extreme that they name: Each row of owner names every owner index once. `left_stats`: every 512 x 512 block is symmetric positive definite. `right_stats`: every 512 x 512 block is symmetric positive definite. `left_roots`: every 512 x 512 block is symmetric. `right_roots`: every 512 x 512 block is symmetric.
All inputs are finite; a program needn't handle non-finite values.
Results may differ from the reference program's by a relative error of at most 0.0003.
Values may be sent and summed in bfloat16 or wider, within the bound.
A program may use at most 64 MiB of HBM per device.

```python
import math
import jax
import jax.numpy as jnp
from jax import lax

BLOCK = 512
MAX_NEWTON = 4
N_REPLICA = 4
N_MP = 4
N_REFRESH = 2


def draw_grad_partial(key, part):
    columns = BLOCK * N_MP
    first = jax.random.fold_in(key, 0)
    base = jnp.clip(jax.random.normal(first, (N_REPLICA, N_REFRESH, BLOCK, columns), jnp.float32), -6.0, 6.0)
    ramp = 1.0 + 2.0 * jnp.arange(N_MP, dtype=jnp.float32) / max(N_MP - 1, 1)
    column_scale = jnp.repeat(ramp, BLOCK)
    values = base
    return (values * column_scale).astype(jnp.bfloat16)


def spd_blocks(key):
    normal = jnp.clip(jax.random.normal(key, (N_REFRESH, N_MP, BLOCK, BLOCK), jnp.float32), -6.0, 6.0)
    gram = jnp.einsum('fmik,fmjk->fmij', normal, normal) * 0.25 + BLOCK * 0.25 * jnp.eye(BLOCK, dtype=jnp.float32)
    return gram.transpose(0, 2, 1, 3).reshape(N_REFRESH, BLOCK, N_MP * BLOCK)


def near_identity(key):
    normal = jnp.clip(jax.random.normal(key, (N_REFRESH, N_MP, BLOCK, BLOCK), jnp.float32), -6.0, 6.0)
    symmetric = (normal + jnp.swapaxes(normal, -1, -2)) * (0.3 / math.sqrt(2.0 * BLOCK))
    roots = 0.25 * (jnp.eye(BLOCK, dtype=jnp.float32) + symmetric)
    return roots.transpose(0, 2, 1, 3).reshape(N_REFRESH, BLOCK, N_MP * BLOCK)


def draw_left_stats(key, part):
    return spd_blocks(jax.random.fold_in(key, 11))


def draw_right_stats(key, part):
    return spd_blocks(jax.random.fold_in(key, 12))


def draw_left_roots(key, part):
    return near_identity(jax.random.fold_in(key, 21))


def draw_right_roots(key, part):
    return near_identity(jax.random.fold_in(key, 22))


def with_ends(values, rng, low, high):
    extent = values.shape
    index_at = [jax.random.randint(jax.random.fold_in(rng, axis), (), 0, extent[axis]) for axis in range(len(extent))]
    values = values.at[tuple(index_at)].set(low)
    longest = extent.index(max(extent))
    index_at[longest] = (index_at[longest] + 1) % extent[longest]
    return values.at[tuple(index_at)].set(high)


def setup_inputs(seed: int = 0) -> dict:
    seeds = jax.random.split(jax.random.key(seed), 8)
    grad_partial = draw_grad_partial(jax.random.fold_in(seeds[7], 71), 0)
    left_stats = draw_left_stats(jax.random.fold_in(seeds[7], 71), 0)
    right_stats = draw_right_stats(jax.random.fold_in(seeds[7], 71), 0)
    left_roots = draw_left_roots(jax.random.fold_in(seeds[7], 71), 0)
    right_roots = draw_right_roots(jax.random.fold_in(seeds[7], 71), 0)
    newton_counts = with_ends(jax.random.randint(seeds[5], (N_REFRESH, N_MP), 1, MAX_NEWTON + 1), jax.random.fold_in(seeds[5], 1), 1, MAX_NEWTON).astype(jnp.int32)
    owner = jax.vmap(lambda own: jax.random.permutation(own, N_MP))(jax.random.split(seeds[6], N_REFRESH)).reshape((N_REFRESH, N_MP)).astype(jnp.int32)
    return dict(grad_partial=grad_partial, left_stats=left_stats, right_stats=right_stats, left_roots=left_roots, right_roots=right_roots, newton_counts=newton_counts, owner=owner)


decay = 0.9
graft_eps = 1e-06

def matmul(left, right):
    return jnp.einsum('nij,njk->nik', left, right, precision=lax.Precision.HIGHEST)

def by_owner(array):
    return array.reshape(N_REFRESH, BLOCK, N_MP, BLOCK).transpose(0, 2, 1, 3).reshape(N_REFRESH * N_MP, BLOCK, BLOCK)

def to_layout(array):
    return array.reshape(N_REFRESH, N_MP, BLOCK, BLOCK).transpose(0, 2, 1, 3).reshape(N_REFRESH, BLOCK, N_MP * BLOCK)

def newton(matrix, counts):
    eye = jnp.eye(BLOCK, dtype=jnp.float32)
    norm = jnp.sqrt(lax.optimization_barrier(jnp.sum(matrix * matrix, axis=(1, 2))))
    scale = 2.5 / norm
    iterate = (scale ** 0.25)[:, None, None] * eye
    coupled = scale[:, None, None] * matrix
    for step_index in range(MAX_NEWTON):
        factor = (5.0 * eye - coupled) * 0.25
        next_iterate = matmul(iterate, factor)
        next_coupled = matmul(matmul(matmul(matmul(coupled, factor), factor), factor), factor)
        live = (step_index < counts)[:, None, None]
        iterate = jnp.where(live, next_iterate, iterate)
        coupled = jnp.where(live, next_coupled, coupled)
    return iterate

def reference(grad_partial, left_stats, right_stats, left_roots, right_roots, newton_counts, owner):
    grad = lax.optimization_barrier(jnp.sum(grad_partial.astype(jnp.float32), axis=0))
    blocks = grad.reshape(N_REFRESH, BLOCK, N_MP, BLOCK).transpose(0, 2, 1, 3)
    inverse = jnp.argsort(owner, axis=1).astype(jnp.int32)
    owned = jnp.take_along_axis(blocks, inverse[:, :, None, None], axis=1).reshape(N_REFRESH * N_MP, BLOCK, BLOCK)
    counts = jnp.take_along_axis(newton_counts, inverse, axis=1).reshape(N_REFRESH * N_MP)
    flipped = jnp.transpose(owned, (0, 2, 1))
    new_left = decay * by_owner(left_stats) + (1.0 - decay) * matmul(owned, flipped)
    new_right = decay * by_owner(right_stats) + (1.0 - decay) * matmul(flipped, owned)
    direction = matmul(matmul(by_owner(left_roots), owned), by_owner(right_roots))
    grad_sq = jnp.sum(owned * owned)
    dir_sq = jnp.sum(direction * direction)
    scaled = direction * (jnp.sqrt(grad_sq) / jnp.sqrt(dir_sq + graft_eps))
    placed = jnp.take_along_axis(scaled.reshape(N_REFRESH, N_MP, BLOCK, BLOCK), owner.astype(jnp.int32)[:, :, None, None], axis=1)
    update = placed.transpose(0, 2, 1, 3).reshape(N_REFRESH, BLOCK, N_MP * BLOCK)
    left_root = newton(new_left, counts)
    right_root = newton(new_right, counts)
    return (update, to_layout(new_left), to_layout(new_right), to_layout(left_root), to_layout(right_root))
```

```python
import functools

import jax
import jax.numpy as jnp
from jax import lax
from jax.experimental import pallas as pl
from jax.experimental.pallas import tpu as pltpu
from jax.sharding import PartitionSpec as P

MAX_NEWTON = 4

decay = 0.9
graft_eps = 1e-06
MESH = pl.DeviceIdType.MESH
F32 = jnp.float32
BF16 = jnp.bfloat16


def split(x):
    hi = x.astype(BF16)
    return hi, (x - hi.astype(F32)).astype(BF16)


def dot(a, b):
    return jnp.dot(a, b, preferred_element_type=F32)


def product(a, b):
    return dot(a[0], b[0]) + (dot(a[0], b[1]) + dot(a[1], b[0]))


def total(x):
    return jnp.sum(jnp.sum(x, axis=0, keepdims=True), axis=1, keepdims=True)


def kernel(
    replicas, owners, groups,
    gp, ls, rs, lr, rr, counts, owner,
    update, new_left, new_right, left_root, right_root,
    routed, part, pieces, g, gt, roots, both, stats, dirs, returned, coupled, factor, factor_s, rows_x, inbox,
    norm_z, norm_m, norm_f,
    a2a_s, a2a_r, st_s, st_r, sc_s, sc_r, ga_s, ga_r, rr_s, rr_r, di_s, di_r, up_s, up_r,
    nz_s, nz_r, nm_s, nm_r, nf_s, nf_r, sw_s, sw_r,
):
    z = lax.axis_index("replica")
    m = lax.axis_index("mp")
    f = lax.axis_index("refresh")
    rows_mp = gp.shape[0]
    order = gp.shape[1] // owners
    rows = order // replicas
    parity = lax.rem(z, 2)
    partner = z + 1 - 2 * parity

    def zpeer(d):
        return lax.rem(z + d, replicas)

    def mpeer(d):
        return lax.rem(m + d, owners)

    def fpeer(d):
        return lax.rem(f + d, groups)

    def zrows(i):
        return pl.ds(pl.multiple_of(i * rows, rows), rows)

    def mrows(i):
        return pl.ds(pl.multiple_of(i * rows_mp, rows_mp), rows_mp)

    sent = []

    def send(src, dst, ssem, rsem, to):
        copy = pltpu.make_async_remote_copy(
            src_ref=src, dst_ref=dst, send_sem=ssem, recv_sem=rsem, device_id=to, device_id_type=MESH
        )
        copy.start()
        sent.append(copy)
        return copy

    barrier = pltpu.get_barrier_semaphore()
    for d in range(1, replicas):
        pl.semaphore_signal(barrier, inc=1, device_id={"replica": zpeer(d)}, device_id_type=MESH)
    for d in range(1, owners):
        pl.semaphore_signal(barrier, inc=1, device_id={"mp": mpeer(d)}, device_id_type=MESH)
    for d in range(1, groups):
        pl.semaphore_signal(barrier, inc=1, device_id={"refresh": fpeer(d)}, device_id_type=MESH)

    def column(o):
        picked = gp[:, 0:order]
        for j in range(1, owners):
            picked = jnp.where(owner[f, j] == o, gp[:, j * order:(j + 1) * order], picked)
        return picked

    for d in range(1, owners):
        routed[d - 1] = column(mpeer(d))
    both[0] = ls[...]
    both[1] = rs[...]
    pl.semaphore_wait(barrier, replicas + owners + groups - 3)

    a2a = [
        send(routed.at[d - 1], part.at[mrows(m)], a2a_s.at[d - 1], a2a_r.at[d - 1], {"mp": mpeer(d)})
        for d in range(1, owners)
    ]
    early = [
        send(both.at[lax.rem(zpeer(d), 2)], stats.at[zrows(z)], st_s.at[d - 1], st_r.at[d - 1],
             {"replica": zpeer(d)})
        for d in range(1, replicas)
    ]
    part[mrows(m), :] = column(m)
    stats[zrows(z), :] = both[parity]
    roots_hi, roots_lo = split(rr[...])
    roots[0, zrows(z), :] = roots_hi
    roots[1, zrows(z), :] = roots_lo
    count = 0
    for j in range(owners):
        count = count + jnp.where(owner[f, j] == m, counts[f, j], 0)

    for copy in a2a:
        copy.wait_recv()
    scatter = [
        send(part.at[zrows(zpeer(d))], pieces.at[d - 1], sc_s.at[d - 1], sc_r.at[d - 1], {"replica": zpeer(d)})
        for d in range(1, replicas)
    ]
    grad = part[zrows(z), :].astype(F32)
    for d in range(1, replicas):
        scatter[d - 1].wait_recv()
        grad = grad + pieces[d - 1].astype(F32)
    grad_hi, grad_lo = split(grad)
    g[0, zrows(z), :] = grad_hi
    g[1, zrows(z), :] = grad_lo
    gather = [
        send(g.at[:, zrows(z), :], g.at[:, zrows(z), :], ga_s.at[d - 1], ga_r.at[d - 1], {"replica": zpeer(d)})
        for d in range(1, replicas)
    ]
    root_sends = [
        send(roots.at[:, zrows(z), :], roots.at[:, zrows(z), :], rr_s.at[d - 1], rr_r.at[d - 1],
             {"replica": zpeer(d)})
        for d in range(1, replicas)
    ]
    grad_sq = total(grad * grad)
    left_slab = split(lr[...])
    for copy in gather:
        copy.wait_recv()
    whole = (g[0], g[1])
    half_dir = split(product(left_slab, whole))
    gt[0] = g[0].T
    gt[1] = g[1].T
    flipped = (gt[0], gt[1])
    new_left[...] = decay * ls[...] + (1.0 - decay) * product((grad_hi, grad_lo), flipped)
    new_right[...] = decay * rs[...] + (1.0 - decay) * product((gt[0, zrows(z), :], gt[1, zrows(z), :]), whole)

    for copy in root_sends:
        copy.wait_recv()
    direction = product(half_dir, (roots[0], roots[1]))
    dirs[zrows(z), :] = direction
    tile = jnp.where(
        lax.broadcasted_iota(jnp.int32, norm_z.shape[1:], 0) < 4, grad_sq, total(direction * direction)
    )
    norm_z[0] = tile
    nz = [
        send(norm_z.at[0], norm_z.at[d], nz_s.at[d - 1], nz_r.at[d - 1], {"replica": zpeer(d)})
        for d in range(1, replicas)
    ]
    spread = [
        send(dirs.at[zrows(z)], dirs.at[zrows(z)], di_s.at[d - 1], di_r.at[d - 1], {"replica": zpeer(d)})
        for d in range(1, replicas)
    ]

    for copy in early:
        copy.wait_recv()
    is_left = parity == 0
    first = tuple(jnp.where(is_left, a, b) for a, b in zip(whole, flipped))
    second = tuple(jnp.where(is_left, b, a) for a, b in zip(whole, flipped))
    chosen = decay * stats[...] + (1.0 - decay) * product(first, second)
    scale = 2.5 / jnp.sqrt(total(chosen * chosen))
    coupled[...] = scale * chosen
    diagonal = lax.broadcasted_iota(jnp.int32, (order, order), 0) == lax.broadcasted_iota(
        jnp.int32, (order, order), 1
    )

    def step(k):
        t = (jnp.where(diagonal, 5.0, 0.0) - coupled[...]) * 0.25
        th, tl = split(t)
        if k == 0:
            factor[...] = t
            root_scale = jnp.sqrt(jnp.sqrt(scale))
            rows_x[0] = root_scale * factor[zrows(partner), :]
            rows_x[1] = root_scale * factor[zrows(z), :]
        else:
            x = rows_x[...].reshape(2 * rows, order)
            nx = product(split(x), (th, tl))
            rows_x[...] = jnp.where(k < count, nx, x).reshape(2, rows, order)
        if k < MAX_NEWTON - 1:
            square = split(product((th, tl), (th, tl)))
            fourth = split(product(square, square))
            coupled[...] = product(split(coupled[...]), fourth)

    step(0)
    for copy in nz:
        copy.wait_recv()
    norms = norm_z[0]
    for d in range(1, replicas):
        norms = norms + norm_z[d]
    norm_m[0] = norms
    nm = [
        send(norm_m.at[0], norm_m.at[d], nm_s.at[d - 1], nm_r.at[d - 1], {"mp": mpeer(d)})
        for d in range(1, owners)
    ]
    step(1)
    for copy in spread:
        copy.wait_recv()
    back = [
        send(dirs.at[mrows(mpeer(d))], returned.at[m], up_s.at[d - 1], up_r.at[d - 1], {"mp": mpeer(d)})
        for d in range(1, owners)
    ]
    returned[m] = dirs[mrows(m), :]
    for copy in nm:
        copy.wait_recv()
    norms = norm_m[0]
    for d in range(1, owners):
        norms = norms + norm_m[d]
    norm_f[0] = norms
    nf = [
        send(norm_f.at[0], norm_f.at[d], nf_s.at[d - 1], nf_r.at[d - 1], {"refresh": fpeer(d)})
        for d in range(1, groups)
    ]
    step(2)
    step(3)
    swap = send(rows_x.at[0], inbox, sw_s.at[0], sw_r.at[0], {"replica": partner})
    for copy in nf:
        copy.wait_recv()
    norms = norm_f[0]
    for d in range(1, groups):
        norms = norms + norm_f[d]
    graft = jnp.sqrt(norms[0:1, 0:1]) / jnp.sqrt(norms[4:5, 0:1] + graft_eps)
    for copy in back:
        copy.wait_recv()
    for j in range(owners):
        picked = returned[0]
        for o in range(1, owners):
            picked = jnp.where(owner[f, j] == o, returned[o], picked)
        update[:, j * order:(j + 1) * order] = picked * graft
    swap.wait_recv()
    own = rows_x[1]
    other = inbox[...]
    left_root[...] = jnp.where(is_left, own, other)
    right_root[...] = jnp.where(is_left, other, own)
    for copy in sent:
        copy.wait_send()


def local(replicas, owners, groups, grad_partial, left_stats, right_stats, left_roots, right_roots, newton_counts, owner):
    rows_mp, columns = grad_partial.shape[2:]
    order = columns // owners
    rows = order // replicas
    vmem = pl.BlockSpec(memory_space=pltpu.VMEM)
    smem = pl.BlockSpec(memory_space=pltpu.SMEM)
    slab = jax.ShapeDtypeStruct((rows, order), F32)
    nz, nm, nf = max(replicas - 1, 1), max(owners - 1, 1), max(groups - 1, 1)
    sems = []
    for n in (nm, nz, nz, nz, nz, nz, nm, nz, nm, nf, 1):
        sems += [pltpu.SemaphoreType.DMA((n,)), pltpu.SemaphoreType.DMA((n,))]
    outs = pl.pallas_call(
        functools.partial(kernel, replicas, owners, groups),
        out_shape=(jax.ShapeDtypeStruct((rows_mp, columns), F32), slab, slab, slab, slab),
        in_specs=[vmem] * 5 + [smem] * 2,
        out_specs=(vmem,) * 5,
        scratch_shapes=[
            pltpu.VMEM((nm, rows_mp, order), BF16),
            pltpu.VMEM((order, order), BF16),
            pltpu.VMEM((nz, rows, order), BF16),
            pltpu.VMEM((2, order, order), BF16),
            pltpu.VMEM((2, order, order), BF16),
            pltpu.VMEM((2, order, order), BF16),
            pltpu.VMEM((2, rows, order), F32),
            pltpu.VMEM((order, order), F32),
            pltpu.VMEM((order, order), F32),
            pltpu.VMEM((owners, rows_mp, order), F32),
            pltpu.VMEM((order, order), F32),
            pltpu.VMEM((order, order), F32),
            pltpu.VMEM((2, order, order), BF16),
            pltpu.VMEM((2, rows, order), F32),
            pltpu.VMEM((rows, order), F32),
            pltpu.VMEM((replicas, 8, 128), F32),
            pltpu.VMEM((owners, 8, 128), F32),
            pltpu.VMEM((groups, 8, 128), F32),
        ] + sems,
        compiler_params=pltpu.CompilerParams(
            collective_id=0, has_side_effects=True, vmem_limit_bytes=48 * 1024 * 1024
        ),
    )(grad_partial[0, 0], left_stats[0], right_stats[0], left_roots[0], right_roots[0], newton_counts, owner)
    return tuple(o[None] for o in outs)


def solution(mesh):
    slabs = P("refresh", "replica", "mp")
    return jax.shard_map(
        functools.partial(local, mesh.shape["replica"], mesh.shape["mp"], mesh.shape["refresh"]),
        mesh=mesh,
        in_specs=(P("replica", "refresh", "mp", None), slabs, slabs, slabs, slabs, P(), P()),
        out_specs=(P("refresh", "mp", None), slabs, slabs, slabs, slabs),
        check_vma=False,
    )
```
